32 devices in a mesh: node: 8 (over z, y), local: 4 (over x, core).
Axes of the slice: x: 2, y: 2, z: 4, core: 2. Of those that a mesh axis runs over, the one named last changes fastest.
Arguments:
- tokens: bfloat16 [2048, 3584], P(('node', 'local')), may hold values from -6 to 6
- expert_ids: int32 [2048, 8], P(('node', 'local')), may hold values from 0 to 15, all different within a row; in each aligned block of 64 rows (0 to 63, 64 to 127, ...) at most 48 rows name the same one
- gate_values: float32 [2048, 8], P(('node', 'local')), may hold values from 0.1 to 1
- holder: int32 [16], replicated, may hold values from 0 to 15, each once
- matching: int32 [8], replicated, may hold values from 0 to 7, as said below
- gate_weight: bfloat16 [32, 3584, 512], P(('node', 'local')), may hold values from -0.09375 to 0.09375
- up_weight: bfloat16 [32, 3584, 512], P(('node', 'local')), may hold values from -0.09375 to 0.09375
- down_weight: bfloat16 [32, 512, 3584], P(('node', 'local')), may hold values from -0.1875 to 0.1875
Outputs:
- moe_out: bfloat16 [2048, 3584], P(('node', 'local'))
- new_gate: bfloat16 [32, 3584, 512], P(('node', 'local'))
- new_up: bfloat16 [32, 3584, 512], P(('node', 'local'))
- new_down: bfloat16 [32, 512, 3584], P(('node', 'local'))
The draws below stay inside these ranges and needn't reach their ends.
Inputs may be any that keep to these rules, and one draw needn't show every extreme that they name: `expert_ids`: each row names 8 different experts. In the 64 rows of one device no expert is named more than 48 times, and some device names some expert exactly 48 times. `holder`: each expert appears once. A perfect matching of the nodes: matching[matching[n]] == n and matching[n] != n.
All inputs are finite; a program needn't handle non-finite values.
Results may differ from the reference program's by a relative error of at most 0.0065.
Values may be sent and summed in bfloat16 or wider, within the bound.
A program may use at most 192 MiB of HBM per device.

```python
import math
import jax
import jax.numpy as jnp
import numpy as np
from jax import lax

D = 3584
FF = 1024
TOP = 8
TOK_DEV = 64
EXPERTS = 16
CAP = 48
TOKENS = 2048
N_NODE = 8
N_LOCAL = 4


def draw_matching(key, part):
    shuffled = jax.random.permutation(key, N_NODE).astype(jnp.int32)
    couples = shuffled.reshape(N_NODE // 2, 2)
    partner = jnp.zeros((N_NODE,), jnp.int32)
    partner = partner.at[couples[:, 0]].set(couples[:, 1])
    partner = partner.at[couples[:, 1]].set(couples[:, 0])
    return partner


def block_scale(own_key, dims, shards, least, largest):
    def one(position, parts):
        draws = jax.random.uniform(jax.random.fold_in(jax.random.fold_in(own_key, 6), position), (parts,), jnp.float32, least / len(shards), largest / len(shards))
        return jnp.repeat(jnp.exp(draws), dims[position] // parts).reshape((-1,) + (1,) * (len(dims) - position - 1))

    loudness = one(*shards[0])
    for cut in shards[1:]:
        loudness = loudness * one(*cut)
    return loudness


def shared_out(own_key, own, number, rows, number_of, top, most, slope):
    ranking = jax.random.permutation(own_key, number_of)
    packed, usual = load_shares(number_of, rows * top, most, slope, True), load_shares(number_of, rows * top, most, slope, False)
    places = jnp.arange(number_of)

    def named(lengths, turn):
        used = int((lengths > 0).sum())
        fixed = max(1, used // 4)
        moved = fixed + (places - fixed + turn * (used - fixed)) % max(1, number_of - fixed)
        return jnp.zeros((number_of,), jnp.int32).at[ranking[jnp.where(places < fixed, places, moved)]].set(jnp.asarray(lengths, jnp.int32))

    lengths = jnp.where(number % 4 == 0, named(packed, number // 4), named(usual, number - number // 4 - 1))
    mixed = jax.random.permutation(jax.random.fold_in(own, 3), number_of)
    source_of, taker = mixed[0:number_of // 2 * 2:2], mixed[1:number_of // 2 * 2:2]
    margin = jnp.minimum(lengths[source_of] - 1, most - lengths[taker]) // 2
    margin = jnp.where((source_of == ranking[0]) | (taker == ranking[0]) | (lengths[taker] == 0), 0, jnp.maximum(margin, 0))
    moved = jax.random.randint(jax.random.fold_in(own, 4), (number_of // 2,), 0, 1 << 20) % (margin + 1)
    lengths = lengths.at[source_of].add(-moved).at[taker].add(moved)
    labels = jnp.searchsorted(jnp.cumsum(lengths), jnp.arange(rows * top), side="right").astype(jnp.int32)
    table = labels.reshape(top, rows).T
    table = table[jax.random.permutation(jax.random.fold_in(own, 1), rows)]
    turn = jax.random.randint(jax.random.fold_in(own, 2), (rows, 1), 0, top)
    return jnp.take_along_axis(table, (jnp.arange(top)[None, :] + turn) % top, axis=1)


def load_shares(amount, total, bound, lean, full):
    portions = [(1 << 20) // math.isqrt(rank ** lean) + 1 for rank in range(1, amount + 1)]
    largest = bound if full else min(bound, max(-(-total // amount), total * portions[0] // sum(portions)))
    least = 1 if total - largest >= amount - 1 else 0
    holding, surplus = [largest] + [least] * (amount - 1), total - largest - least * (amount - 1)
    while surplus > 0:
        candidates = [i for i in range(1, amount) if holding[i] < largest] or [i for i in range(1, amount) if holding[i] < bound]
        mass, budget = sum([portions[i] for i in candidates]), surplus
        for i in candidates:
            extra = min(bound - holding[i], max(1, budget * portions[i] // mass), surplus)
            holding[i] = holding[i] + extra
            surplus = surplus - extra
    return np.array(holding)


def centred(rng, shape, deviation, limit, cuts=(), kind=jnp.bfloat16):
    values = deviation * jax.random.normal(rng, shape, jnp.float32)
    if cuts:
        values = values * block_scale(rng, shape, cuts, -0.22, 0.18)
    return jnp.clip(values, -limit, limit).astype(kind)


def setup_inputs(seed: int = 0) -> dict:
    seeds = jax.random.split(jax.random.key(seed), 9)
    tokens = centred(seeds[0], (TOKENS, D), 1.0, 6.0, ((0, 32),))
    expert_ids_keys = jax.random.split(jax.random.fold_in(seeds[1], 1), TOKENS // TOK_DEV)
    expert_ids_turns = jax.random.permutation(jax.random.fold_in(seeds[1], 3), TOKENS // TOK_DEV)
    expert_ids = jax.vmap(lambda own, number: shared_out(jax.random.fold_in(seeds[1], 2), own, number, TOK_DEV, EXPERTS, TOP, CAP, 2))(expert_ids_keys, expert_ids_turns).reshape((TOKENS, TOP))
    gate_values = jnp.clip(0.1 + 0.9 * jax.random.uniform(seeds[2], (TOKENS, TOP), jnp.float32) ** block_scale(seeds[2], (TOKENS, TOP), ((0, 32),), -0.2, 0.2), 0.1, 1.0)
    holder = jax.random.permutation(seeds[3], EXPERTS).astype(jnp.int32)
    matching = draw_matching(jax.random.fold_in(seeds[8], 71), 0)
    gate_weight = centred(seeds[5], (2 * EXPERTS, D, FF // 2), D ** -0.5, 0.09375, ((0, 32),))
    up_weight = centred(seeds[6], (2 * EXPERTS, D, FF // 2), D ** -0.5, 0.09375, ((0, 32),))
    down_weight = centred(seeds[7], (2 * EXPERTS, FF // 2, D), FF ** -0.5, 0.1875, ((0, 32),))
    return dict(tokens=tokens, expert_ids=expert_ids, gate_values=gate_values, holder=holder, matching=matching, gate_weight=gate_weight, up_weight=up_weight, down_weight=down_weight)


def reference(tokens, expert_ids, gate_values, holder, matching, gate_weight, up_weight, down_weight):
    row_limit = N_NODE * N_LOCAL * CAP
    expert_range = jnp.arange(EXPERTS, dtype=jnp.int32)
    slot_of_expert = jnp.zeros((EXPERTS,), jnp.int32).at[holder].set(expert_range)
    flat_expert = expert_ids.reshape(-1)
    flat_gate = gate_values.reshape(-1)
    sorted_routes = jnp.argsort(flat_expert, stable=True).astype(jnp.int32)
    counts = jnp.sum((flat_expert[:, None] == expert_range[None, :]).astype(jnp.int32), axis=0)
    starts = (jnp.cumsum(counts) - counts).astype(jnp.int32)
    padded_order = jnp.concatenate([sorted_routes, jnp.zeros((row_limit,), jnp.int32)])
    running = jnp.zeros((TOKENS, D), jnp.float32)

    def accumulate(running, expert):
        picked = lax.dynamic_slice(padded_order, (starts[expert],), (row_limit,))
        is_live = jnp.arange(row_limit) < counts[expert]
        token_index = (picked // TOP).astype(jnp.int32)
        row_block = tokens[token_index]
        slot_here = slot_of_expert[expert]
        result = jnp.zeros((row_limit, D), jnp.float32)
        for part_index in range(2):
            row_index = 2 * slot_here + part_index
            gate_proj = jnp.dot(row_block, gate_weight[row_index], preferred_element_type=jnp.float32)
            up_proj = jnp.dot(row_block, up_weight[row_index], preferred_element_type=jnp.float32)
            hidden = (jax.nn.silu(gate_proj) * up_proj).astype(jnp.bfloat16)
            partial_value = jnp.dot(hidden, down_weight[row_index], preferred_element_type=jnp.float32).astype(jnp.bfloat16)
            result = result + partial_value.astype(jnp.float32)
        output = result.astype(jnp.bfloat16).astype(jnp.float32)
        weight = jnp.where(is_live, flat_gate[picked], 0.0)
        running = running.at[token_index].add(weight[:, None] * output)
        return running, None

    running, ignored = lax.scan(accumulate, running, expert_range)
    combined = running.astype(jnp.bfloat16)

    def reorder(matrix):
        grouped = matrix.reshape((N_NODE, matrix.shape[0] // N_NODE) + matrix.shape[1:])
        return grouped[matching].reshape(matrix.shape)

    return combined, reorder(gate_weight), reorder(up_weight), reorder(down_weight)
```

```python
import jax
import jax.numpy as jnp
import numpy as np
from jax import lax
from jax.sharding import PartitionSpec as P


def perfect_matchings(nodes):
    if not nodes:
        return [[]]
    first = nodes[0]
    found = []
    for other in nodes[1:]:
        rest = [n for n in nodes if n not in (first, other)]
        for tail in perfect_matchings(rest):
            found.append([(first, other)] + tail)
    return found


def matching_count(node_count):
    count = 1
    for odd in range(1, node_count, 2):
        count *= odd
    return count


def move_by_all_to_all(part, matching):
    node_count = lax.axis_size("node")
    pieces = part.reshape((node_count, part.shape[1] // node_count, part.shape[2]))
    arrived = lax.all_to_all(pieces, "node", split_axis=0, concat_axis=0, tiled=True)
    reordered = jnp.take(arrived, matching, axis=0)
    returned = lax.all_to_all(reordered, "node", split_axis=0, concat_axis=0, tiled=True)
    return returned.reshape(part.shape)


def matching_number(matching, table):
    same = jnp.all(jnp.asarray(table) == matching[None, :], axis=1)
    return jnp.sum(jnp.where(same, jnp.arange(table.shape[0], dtype=jnp.int32), 0))


def matching_table(node_count):
    couples = perfect_matchings(list(range(node_count)))
    table = np.zeros((len(couples), node_count), np.int32)
    for row, pairs in enumerate(couples):
        for a, b in pairs:
            table[row, a] = b
            table[row, b] = a
    return table


def move_weights(weights, matching):
    node_count = lax.axis_size("node")
    if matching_count(node_count) > 128:
        return tuple(move_by_all_to_all(part, matching) for part in weights)
    table = matching_table(node_count)

    def branch(row):
        pairs = [(int(table[row, n]), n) for n in range(node_count)]
        return lambda *parts: tuple(lax.ppermute(p, "node", pairs) for p in parts)

    branches = [branch(row) for row in range(table.shape[0])]
    return lax.switch(matching_number(matching, table), branches, *weights)


def per_device(
    tokens, expert_ids, gate_values, holder, matching, gate_weight, up_weight, down_weight
):
    gather_axes = ("local", "node")
    own = jnp.sum(
        jnp.where(expert_ids[:, :, None] == holder[None, None, :], gate_values[:, :, None], 0.0),
        axis=1,
    )
    all_gates = lax.all_gather(own, gather_axes, axis=0, tiled=True)
    rows = lax.all_gather(tokens, gather_axes, axis=0, tiled=True)
    (new_gate,) = move_weights((gate_weight,), matching)
    rows, new_gate = lax.optimization_barrier((rows, new_gate))
    slot = (lax.axis_index("node") * lax.axis_size("local") + lax.axis_index("local")) // 2
    share = lax.dynamic_slice_in_dim(all_gates, slot, 1, axis=1)
    gate_proj = jnp.dot(rows, gate_weight[0], preferred_element_type=jnp.float32)
    up_proj = jnp.dot(rows, up_weight[0], preferred_element_type=jnp.float32)
    hidden = (jax.nn.silu(gate_proj) * up_proj * share).astype(jnp.bfloat16)
    partial_value = jnp.dot(hidden, down_weight[0], preferred_element_type=jnp.float32)
    partial_value = partial_value.astype(jnp.bfloat16)
    partial_value, later_matching = lax.optimization_barrier((partial_value, matching))
    summed = lax.psum_scatter(partial_value, "local", scatter_dimension=0, tiled=True)
    combined = lax.psum_scatter(summed, "node", scatter_dimension=0, tiled=True)
    new_up, new_down = move_weights((up_weight, down_weight), later_matching)
    return (combined, new_gate, new_up, new_down)


def solution(mesh):
    in_specs = (
        P(("node", "local"), None),
        P(("node", "local"), None),
        P(("node", "local"), None),
        P(),
        P(),
        P(("node", "local"), None, None),
        P(("node", "local"), None, None),
        P(("node", "local"), None, None),
    )
    out_specs = (
        P(("node", "local"), None),
        P(("node", "local"), None, None),
        P(("node", "local"), None, None),
        P(("node", "local"), None, None),
    )
    return jax.shard_map(
        per_device, mesh=mesh, in_specs=in_specs, out_specs=out_specs, check_vma=False
    )
```

```python
import jax
import jax.numpy as jnp
import numpy as np
from jax import lax
from jax.sharding import PartitionSpec as P


def perfect_matchings(nodes):
    if not nodes:
        return [[]]
    first = nodes[0]
    found = []
    for other in nodes[1:]:
        rest = [n for n in nodes if n not in (first, other)]
        for tail in perfect_matchings(rest):
            found.append([(first, other)] + tail)
    return found


def matching_count(node_count):
    count = 1
    for odd in range(1, node_count, 2):
        count *= odd
    return count


def move_by_all_to_all(part, matching):
    node_count = lax.axis_size("node")
    pieces = part.reshape((node_count, part.shape[1] // node_count, part.shape[2]))
    arrived = lax.all_to_all(pieces, "node", split_axis=0, concat_axis=0, tiled=True)
    reordered = jnp.take(arrived, matching, axis=0)
    returned = lax.all_to_all(reordered, "node", split_axis=0, concat_axis=0, tiled=True)
    return returned.reshape(part.shape)


def matching_number(matching, table):
    same = jnp.all(jnp.asarray(table) == matching[None, :], axis=1)
    return jnp.sum(jnp.where(same, jnp.arange(table.shape[0], dtype=jnp.int32), 0))


def matching_table(node_count):
    couples = perfect_matchings(list(range(node_count)))
    table = np.zeros((len(couples), node_count), np.int32)
    for row, pairs in enumerate(couples):
        for a, b in pairs:
            table[row, a] = b
            table[row, b] = a
    return table


def move_weights(weights, matching):
    node_count = lax.axis_size("node")
    if matching_count(node_count) > 128:
        return tuple(move_by_all_to_all(part, matching) for part in weights)
    table = matching_table(node_count)

    def branch(row):
        pairs = [(int(table[row, n]), n) for n in range(node_count)]
        return lambda *parts: tuple(lax.ppermute(p, "node", pairs) for p in parts)

    branches = [branch(row) for row in range(table.shape[0])]
    return lax.switch(matching_number(matching, table), branches, *weights)


def per_device(
    tokens, expert_ids, gate_values, holder, matching, gate_weight, up_weight, down_weight
):
    gather_axes = ("local", "node")
    own = jnp.sum(
        jnp.where(expert_ids[:, :, None] == holder[None, None, :], gate_values[:, :, None], 0.0),
        axis=1,
    )
    rows = lax.all_gather(tokens, gather_axes, axis=0, tiled=True)
    (new_gate,) = move_weights((gate_weight,), matching)
    rows, new_gate, own = lax.optimization_barrier((rows, new_gate, own))
    all_gates = lax.all_gather(own, gather_axes, axis=0, tiled=True)
    slot = (lax.axis_index("node") * lax.axis_size("local") + lax.axis_index("local")) // 2
    share = lax.dynamic_slice_in_dim(all_gates, slot, 1, axis=1)
    gate_proj = jnp.dot(rows, gate_weight[0], preferred_element_type=jnp.float32)
    up_proj = jnp.dot(rows, up_weight[0], preferred_element_type=jnp.float32)
    hidden = (jax.nn.silu(gate_proj) * up_proj * share).astype(jnp.bfloat16)
    partial_value = jnp.dot(hidden, down_weight[0], preferred_element_type=jnp.float32)
    partial_value = partial_value.astype(jnp.bfloat16)
    partial_value, up_matching = lax.optimization_barrier((partial_value, matching))
    summed = lax.psum_scatter(partial_value, "local", scatter_dimension=0, tiled=True)
    (new_up,) = move_weights((up_weight,), up_matching)
    summed, new_up, down_matching = lax.optimization_barrier((summed, new_up, matching))
    combined = lax.psum_scatter(summed, "node", scatter_dimension=0, tiled=True)
    (new_down,) = move_weights((down_weight,), down_matching)
    return (combined, new_gate, new_up, new_down)


def solution(mesh):
    in_specs = (
        P(("node", "local"), None),
        P(("node", "local"), None),
        P(("node", "local"), None),
        P(),
        P(),
        P(("node", "local"), None, None),
        P(("node", "local"), None, None),
        P(("node", "local"), None, None),
    )
    out_specs = (
        P(("node", "local"), None),
        P(("node", "local"), None, None),
        P(("node", "local"), None, None),
        P(("node", "local"), None, None),
    )
    return jax.shard_map(
        per_device, mesh=mesh, in_specs=in_specs, out_specs=out_specs, check_vma=False
    )
```

```python
import jax
import jax.numpy as jnp
import numpy as np
from jax import lax
from jax.sharding import PartitionSpec as P


def perfect_matchings(nodes):
    if not nodes:
        return [[]]
    first = nodes[0]
    found = []
    for other in nodes[1:]:
        rest = [n for n in nodes if n not in (first, other)]
        for tail in perfect_matchings(rest):
            found.append([(first, other)] + tail)
    return found


def matching_count(node_count):
    count = 1
    for odd in range(1, node_count, 2):
        count *= odd
    return count


def move_by_all_to_all(part, matching):
    node_count = lax.axis_size("node")
    pieces = part.reshape((node_count, part.shape[1] // node_count, part.shape[2]))
    arrived = lax.all_to_all(pieces, "node", split_axis=0, concat_axis=0, tiled=True)
    reordered = jnp.take(arrived, matching, axis=0)
    returned = lax.all_to_all(reordered, "node", split_axis=0, concat_axis=0, tiled=True)
    return returned.reshape(part.shape)


def matching_number(matching, table):
    same = jnp.all(jnp.asarray(table) == matching[None, :], axis=1)
    return jnp.sum(jnp.where(same, jnp.arange(table.shape[0], dtype=jnp.int32), 0))


def matching_table(node_count):
    couples = perfect_matchings(list(range(node_count)))
    table = np.zeros((len(couples), node_count), np.int32)
    for row, pairs in enumerate(couples):
        for a, b in pairs:
            table[row, a] = b
            table[row, b] = a
    return table


def move_weights(weights, matching):
    node_count = lax.axis_size("node")
    if matching_count(node_count) > 128:
        return tuple(move_by_all_to_all(part, matching) for part in weights)
    table = matching_table(node_count)

    def branch(row):
        pairs = [(int(table[row, n]), n) for n in range(node_count)]
        return lambda *parts: tuple(lax.ppermute(p, "node", pairs) for p in parts)

    branches = [branch(row) for row in range(table.shape[0])]
    return lax.switch(matching_number(matching, table), branches, *weights)


def per_device(
    tokens, expert_ids, gate_values, holder, matching, gate_weight, up_weight, down_weight
):
    gather_axes = ("local", "node")
    own = jnp.sum(
        jnp.where(expert_ids[:, :, None] == holder[None, None, :], gate_values[:, :, None], 0.0),
        axis=1,
    )
    features, experts = tokens.shape[1], holder.shape[0]
    high = lax.reduce_precision(own, 8, 7)
    low = lax.reduce_precision(own - high, 8, 7)
    padding = jnp.zeros((tokens.shape[0], -(2 * experts) % 128), jnp.bfloat16)
    sent = jnp.concatenate(
        [tokens, high.astype(jnp.bfloat16), low.astype(jnp.bfloat16), padding], axis=1
    )
    arrived = lax.all_gather(sent, gather_axes, axis=0, tiled=True)
    (new_gate,) = move_weights((gate_weight,), matching)
    arrived, new_gate = lax.optimization_barrier((arrived, new_gate))
    rows = arrived[:, :features]
    slot = (lax.axis_index("node") * lax.axis_size("local") + lax.axis_index("local")) // 2
    terms = arrived[:, features : features + 2 * experts].astype(jnp.float32)
    share = lax.dynamic_slice_in_dim(terms, slot, 1, axis=1)
    share = share + lax.dynamic_slice_in_dim(terms, experts + slot, 1, axis=1)
    gate_proj = jnp.dot(rows, gate_weight[0], preferred_element_type=jnp.float32)
    up_proj = jnp.dot(rows, up_weight[0], preferred_element_type=jnp.float32)
    hidden = (jax.nn.silu(gate_proj) * up_proj * share).astype(jnp.bfloat16)
    partial_value = jnp.dot(hidden, down_weight[0], preferred_element_type=jnp.float32)
    partial_value = partial_value.astype(jnp.bfloat16)
    partial_value, up_matching = lax.optimization_barrier((partial_value, matching))
    summed = lax.psum_scatter(partial_value, "local", scatter_dimension=0, tiled=True)
    (new_up,) = move_weights((up_weight,), up_matching)
    summed, new_up, down_matching = lax.optimization_barrier((summed, new_up, matching))
    combined = lax.psum_scatter(summed, "node", scatter_dimension=0, tiled=True)
    (new_down,) = move_weights((down_weight,), down_matching)
    return (combined, new_gate, new_up, new_down)


def solution(mesh):
    in_specs = (
        P(("node", "local"), None),
        P(("node", "local"), None),
        P(("node", "local"), None),
        P(),
        P(),
        P(("node", "local"), None, None),
        P(("node", "local"), None, None),
        P(("node", "local"), None, None),
    )
    out_specs = (
        P(("node", "local"), None),
        P(("node", "local"), None, None),
        P(("node", "local"), None, None),
        P(("node", "local"), None, None),
    )
    return jax.shard_map(
        per_device, mesh=mesh, in_specs=in_specs, out_specs=out_specs, check_vma=False
    )
```
